32 devices in a mesh: dp: 4 (over y, x), tensor: 8 (over z, core).
Axes of the slice: x: 2, y: 2, z: 4, core: 2. Of those that a mesh axis runs over, the one named last changes fastest.
Arguments:
- inputs: bfloat16 [3072, 4096], P('dp', 'tensor'), may hold values from -6 to 6
- cotangent: bfloat16 [3072, 4096], P('dp', 'tensor'), may hold values from -0.059814453 to 0.059814453
- gate_pre: bfloat16 [3072, 18432], P('dp', 'tensor'), may hold values from -6 to 6
- up_pre: bfloat16 [3072, 18432], P('dp', 'tensor'), may hold values from -6 to 6
- down_weight: bfloat16 [18432, 4096], P('tensor'), may hold values from -0.046875 to 0.046875
- gate_a: bfloat16 [4096, 64], P('tensor'), may hold values from -0.09375 to 0.09375
- gate_b: bfloat16 [64, 18432], P(None, 'tensor'), may hold values from -0.75 to 0.75
- up_a: bfloat16 [4096, 64], P('tensor'), may hold values from -0.09375 to 0.09375
- up_b: bfloat16 [64, 18432], P(None, 'tensor'), may hold values from -0.75 to 0.75
- down_a: bfloat16 [18432, 64], P('tensor'), may hold values from -0.046875 to 0.046875
- down_adapter_second: bfloat16 [64, 4096], P(None, 'tensor'), may hold values from -0.75 to 0.75
Outputs:
- gate_first_gradient: float32 [4096, 64], P('tensor')
- gate_second_gradient: float32 [64, 18432], P(None, 'tensor')
- up_first_gradient: float32 [4096, 64], P('tensor')
- up_second_gradient: float32 [64, 18432], P(None, 'tensor')
- grad_down_a: float32 [18432, 64], P('tensor')
- down_second_gradient: float32 [64, 4096], P(None, 'tensor')
The draws below stay inside these ranges and needn't reach their ends.
All inputs are finite; a program needn't handle non-finite values.
Results may differ from the reference program's by a relative error of at most 0.005.
Values may be sent and summed in bfloat16 or wider, within the bound.
No kernel may reach another device: no remote copies, remote signals or barrier semaphores. Data moves between devices by JAX's collectives and lax.ppermute only.
A program may use at most 128 MiB of HBM per device.

```python
import jax
import jax.numpy as jnp

D = 4096
FF = 18432
R = 64
TOKENS = 3072


def block_scale(rng, shape, split, low, largest):
    def one(axis_at, shards_of):
        steps = jax.random.uniform(jax.random.fold_in(jax.random.fold_in(rng, 6), axis_at), (shards_of,), jnp.float32, low / len(split), largest / len(split))
        return jnp.repeat(jnp.exp(steps), shape[axis_at] // shards_of).reshape((-1,) + (1,) * (len(shape) - axis_at - 1))

    gain = one(*split[0])
    for cut in split[1:]:
        gain = gain * one(*cut)
    return gain


def scatter_about(rng, shape, width, most, pieces=(), kind=jnp.bfloat16):
    drawn = jax.random.normal(rng, shape, jnp.float32) * width
    if len(pieces) > 0:
        drawn = block_scale(rng, shape, pieces, -0.22, 0.18) * drawn
    return jnp.clip(drawn, min=-most, max=most).astype(kind)


def setup_inputs(seed: int = 0) -> dict:
    seeds = jax.random.split(jax.random.key(seed), 12)
    inputs = scatter_about(seeds[0], (TOKENS, D), 1.0, 6.0, ((0, 4), (1, 8)))
    cotangent = scatter_about(seeds[1], (TOKENS, D), 0.01, 0.059814453, ((0, 4), (1, 8)))
    gate_pre = scatter_about(seeds[2], (TOKENS, FF), 1.0, 6.0, ((0, 4), (1, 8)))
    up_pre = scatter_about(seeds[3], (TOKENS, FF), 1.0, 6.0, ((0, 4), (1, 8)))
    down_weight = scatter_about(seeds[4], (FF, D), FF ** -0.5, 0.046875, ((0, 8),))
    gate_a = scatter_about(seeds[5], (D, R), D ** -0.5, 0.09375, ((0, 8),))
    gate_b = scatter_about(seeds[6], (R, FF), R ** -0.5, 0.75, ((1, 8),))
    up_a = scatter_about(seeds[7], (D, R), D ** -0.5, 0.09375, ((0, 8),))
    up_b = scatter_about(seeds[8], (R, FF), R ** -0.5, 0.75, ((1, 8),))
    down_a = scatter_about(seeds[9], (FF, R), FF ** -0.5, 0.046875, ((0, 8),))
    down_adapter_second = scatter_about(seeds[10], (R, D), R ** -0.5, 0.75, ((1, 8),))
    return {"inputs": inputs, "cotangent": cotangent, "gate_pre": gate_pre, "up_pre": up_pre, "down_weight": down_weight, "gate_a": gate_a, "gate_b": gate_b, "up_a": up_a, "up_b": up_b, "down_a": down_a, "down_adapter_second": down_adapter_second}


adapter_scale_factor = 2.0


def silu_parts(pre):
    sigma = jax.nn.sigmoid(pre)
    return pre * sigma, sigma * (1.0 + pre * (1.0 - sigma))


def matrix_multiply(left, right):
    return jnp.dot(left, right, preferred_element_type=jnp.float32)


def reference(inputs, cotangent, gate_pre, up_pre, down_weight, gate_a, gate_b, up_a, up_b, down_a, down_adapter_second):
    gate_wide = gate_pre.astype(jnp.float32)
    up_wide = up_pre.astype(jnp.float32)
    active, slope = silu_parts(gate_wide)
    hidden = (active * up_wide).astype(jnp.bfloat16)
    gate_reduced_rank = matrix_multiply(inputs, gate_a).astype(jnp.bfloat16)
    up_reduced_rank = matrix_multiply(inputs, up_a).astype(jnp.bfloat16)
    down_reduced_rank = matrix_multiply(hidden, down_a).astype(jnp.bfloat16)
    down_backward = (adapter_scale_factor * matrix_multiply(cotangent, down_adapter_second.T)).astype(jnp.bfloat16)
    hidden_grad = matrix_multiply(cotangent, down_weight.T) + matrix_multiply(down_backward, down_a.T)
    gate_gradient = (hidden_grad * up_wide * slope).astype(jnp.bfloat16)
    up_gradient = (hidden_grad * active).astype(jnp.bfloat16)
    gate_backward = matrix_multiply(gate_gradient, gate_b.T).astype(jnp.bfloat16)
    up_backward = matrix_multiply(up_gradient, up_b.T).astype(jnp.bfloat16)
    gate_second_gradient = adapter_scale_factor * matrix_multiply(gate_reduced_rank.T, gate_gradient)
    up_second_gradient = adapter_scale_factor * matrix_multiply(up_reduced_rank.T, up_gradient)
    gate_first_gradient = adapter_scale_factor * matrix_multiply(inputs.T, gate_backward)
    up_first_gradient = adapter_scale_factor * matrix_multiply(inputs.T, up_backward)
    grad_down_a = matrix_multiply(hidden.T, down_backward)
    down_second_gradient = adapter_scale_factor * matrix_multiply(down_reduced_rank.T, cotangent)
    return (gate_first_gradient, gate_second_gradient, up_first_gradient, up_second_gradient, grad_down_a, down_second_gradient)
```

```python
import functools

import jax
import jax.numpy as jnp
from jax import lax
from jax.experimental import pallas as pl
from jax.experimental.pallas import tpu as pltpu
from jax.sharding import PartitionSpec as P

adapter_scale_factor = 2.0
LANES = 128
BF = jnp.bfloat16
F32 = jnp.float32


def silu_parts(pre):
    sigma = 0.5 + 0.5 * jnp.tanh(0.5 * pre)
    return pre * sigma, sigma * (1.0 + pre * (1.0 - sigma))


def dot_nt(left, right):
    return lax.dot_general(left, right, (((1,), (1,)), ((), ())), preferred_element_type=F32)


def dot_nn(left, right):
    return jnp.dot(left, right, preferred_element_type=F32)


def dot_tn(left, right):
    return lax.dot_general(left, right, (((0,), (0,)), ((), ())), preferred_element_type=F32)


def pin(x, *after):
    return lax.optimization_barrier((x, *after))[0]


def divisor(size, most):
    best = LANES
    for width in range(LANES, most + 1, LANES):
        if size % width == 0:
            best = width
    return best


def cost(flops, moved, transcendentals=0):
    return pl.CostEstimate(flops=flops, bytes_accessed=moved, transcendentals=transcendentals)


def grad_kernel(n_blocks, has_acc, finish, first, final, *refs):
    blocks = refs[2 : 2 + n_blocks]
    weights = refs[2 + n_blocks : 2 + 2 * n_blocks]
    refs = refs[2 + 2 * n_blocks :]
    grad = dot_nt(blocks[0][...], weights[0][...])
    for block, w_ref in zip(blocks[1:], weights[1:]):
        grad = grad + dot_nt(block[...], w_ref[...])
    if has_acc:
        grad = grad + refs[0][...]
        refs = refs[1:]
    if not finish:
        refs[0][...] = grad
        return
    back_ref, da_ref, factor_ref, act_ref, gb_ref, ub_ref, low_ref = refs[:7]
    part_ref = refs[-3 if final else -2]
    step = pl.program_id(0)
    grad = grad + dot_tn(back_ref[...], da_ref[...])
    gate_grad = (grad * factor_ref[...]).astype(BF)
    up_grad = (grad * act_ref[...]).astype(BF)
    zeros = jnp.zeros_like(gb_ref)
    part = dot_nt(gate_grad, jnp.concatenate([gb_ref[...], zeros], axis=0))
    part = part + dot_nt(up_grad, jnp.concatenate([zeros, ub_ref[...]], axis=0))

    @pl.when(step == 0)
    def _():
        part_ref[...] = part

    @pl.when(step > 0)
    def _():
        part_ref[...] += part

    rank = low_ref.shape[0] // 2
    gate_second = dot_nn(low_ref[:rank, :], gate_grad)
    up_second = dot_nn(low_ref[rank:, :], up_grad)
    if not first:
        gate_second = refs[7][:rank, :] + gate_second
        up_second = refs[7][rank:, :] + up_second
    if final:
        refs[-2][...] = gate_second.astype(BF)
        refs[-1][...] = up_second.astype(BF)
    else:
        refs[-1][:rank, :] = gate_second
        refs[-1][rank:, :] = up_second


def grad_call(name, span, table, me, pieces, weight, acc, rest=None, second=None, final=False):
    at, size = span
    index = at // size
    hidden = weight.shape[0]
    blocks = [block for _, block in pieces]
    width = blocks[0].shape[1]
    tile = divisor(hidden, 768)
    finish = rest is not None
    per = int(round(table.shape[0] ** 0.5))
    in_specs = [pl.BlockSpec((size, width), lambda j, t, m: (0, 0)) for _ in blocks]
    for column, _ in pieces:
        in_specs.append(
            pl.BlockSpec(
                (tile, width), lambda j, t, m, column=column: (j, t[m[0] * per + column])
            )
        )
    args = [*blocks, *[weight] * len(blocks)]
    if acc is not None:
        in_specs.append(pl.BlockSpec((size, tile), lambda j, t, m: (index, j)))
        args.append(acc)
    flops = 2 * size * hidden * width * len(blocks)
    moved = 2 * hidden * width * len(blocks) + 8 * size * hidden
    if finish:
        back, low = rest[0], rest[-1]
        ranks = low.shape[0]
        rank = ranks // 2
        flops += 2 * size * hidden * 8 * ranks
        in_specs += [
            pl.BlockSpec((rank, size), lambda j, t, m: (0, index)),
            pl.BlockSpec((rank, tile), lambda j, t, m: (0, j)),
            pl.BlockSpec((size, tile), lambda j, t, m: (index, j)),
            pl.BlockSpec((size, tile), lambda j, t, m: (index, j)),
            pl.BlockSpec((rank, tile), lambda j, t, m: (0, j)),
            pl.BlockSpec((rank, tile), lambda j, t, m: (0, j)),
            pl.BlockSpec((ranks, size), lambda j, t, m: (0, index)),
        ]
        args += rest
        if second is not None:
            in_specs.append(pl.BlockSpec((ranks, tile), lambda j, t, m: (0, j)))
            args.append(second)
        out_specs = [pl.BlockSpec((size, ranks), lambda j, t, m: (0, 0))]
        out_shape = [jax.ShapeDtypeStruct((size, ranks), F32)]
        if final:
            out_specs += [pl.BlockSpec((rank, tile), lambda j, t, m: (0, j))] * 2
            out_shape += [jax.ShapeDtypeStruct((rank, hidden), BF)] * 2
        else:
            out_specs.append(pl.BlockSpec((ranks, tile), lambda j, t, m: (0, j)))
            out_shape.append(jax.ShapeDtypeStruct((ranks, hidden), F32))
    else:
        out_specs = pl.BlockSpec((size, tile), lambda j, t, m: (0, j))
        out_shape = jax.ShapeDtypeStruct((size, hidden), F32)
    return pl.pallas_call(
        functools.partial(
            grad_kernel, len(blocks), acc is not None, finish, second is None, final
        ),
        grid_spec=pltpu.PrefetchScalarGridSpec(
            num_scalar_prefetch=2,
            grid=(hidden // tile,),
            in_specs=in_specs,
            out_specs=out_specs,
        ),
        out_shape=out_shape,
        compiler_params=pltpu.CompilerParams(vmem_limit_bytes=36 * 1024 * 1024),
        cost_estimate=cost(flops, moved),
        name=name,
    )(table, me, *args)


def low_kernel(x_ref, ga_ref, ua_ref, cot_ref, s_ref, low_ref):
    rank = s_ref.shape[0]
    both = jnp.concatenate([ga_ref[...], ua_ref[...]], axis=0)
    low_ref[: 2 * rank, :] = dot_nt(x_ref[...], both).T
    back = adapter_scale_factor * dot_nt(cot_ref[...], s_ref[...])
    low_ref[2 * rank :, :] = back.T


def low_call(inputs, ga, ua, cotangent, second):
    return pl.pallas_call(
        low_kernel,
        out_shape=jax.ShapeDtypeStruct((3 * second.shape[0], inputs.shape[0]), F32),
        compiler_params=pltpu.CompilerParams(vmem_limit_bytes=60 * 1024 * 1024),
        cost_estimate=cost(1024, 1024),
        name="low",
    )(inputs, ga, ua, cotangent, second)


def hidden_kernel(gate_ref, up_ref, da_ref, down_ref, hidden_ref, factor_ref, act_ref, acc_ref):
    step = pl.program_id(0)
    up = up_ref[...].astype(F32)
    act, slope = silu_parts(gate_ref[...].astype(F32))
    factor_ref[...] = up * slope
    act_ref[...] = act
    hidden = (act * up).astype(BF)
    hidden_ref[...] = hidden
    part = dot_nt(hidden, da_ref[...])

    @pl.when(step == 0)
    def _():
        acc_ref[...] = part

    @pl.when(step > 0)
    def _():
        acc_ref[...] += part

    @pl.when(step == pl.num_programs(0) - 1)
    def _():
        turned = acc_ref[...].T
        rank = turned.shape[0]
        for i in range(turned.shape[1] // LANES):
            down_ref[i * rank : (i + 1) * rank, :] = turned[:, i * LANES : (i + 1) * LANES]


def hidden_call(gate_pre, up_pre, da):
    tokens, hidden = gate_pre.shape
    rank = da.shape[0]
    tile = divisor(hidden, 384)
    rows = rank * tokens // LANES
    wide = pl.BlockSpec((tokens, tile), lambda j: (0, j))
    return pl.pallas_call(
        hidden_kernel,
        grid=(hidden // tile,),
        in_specs=[wide, wide, pl.BlockSpec((rank, tile), lambda j: (0, j))],
        out_specs=[pl.BlockSpec((rows, LANES), lambda j: (0, 0)), wide, wide, wide],
        out_shape=[
            jax.ShapeDtypeStruct((rows, LANES), F32),
            jax.ShapeDtypeStruct((tokens, hidden), BF),
            jax.ShapeDtypeStruct((tokens, hidden), F32),
            jax.ShapeDtypeStruct((tokens, hidden), F32),
        ],
        scratch_shapes=[pltpu.VMEM((tokens, rank), F32)],
        compiler_params=pltpu.CompilerParams(vmem_limit_bytes=60 * 1024 * 1024),
        cost_estimate=cost(1024, 1024),
        name="hidden",
    )(gate_pre, up_pre, da)


def packed(x, plain):
    upper = lax.reduce_precision(x[plain:], exponent_bits=8, mantissa_bits=7)
    rest = x[plain:] - upper
    return jnp.concatenate([x[:plain], upper, rest], axis=0).astype(BF)


def unpacked(x, plain):
    x = x.astype(F32)
    end = (plain + x.shape[0]) // 2
    return jnp.concatenate([x[:plain], x[plain:end] + x[end:]], axis=0)


def summed(values):
    total = values[0].astype(F32)
    for value in values[1:]:
        total = total + value.astype(F32)
    return total


class Places:
    def __init__(self, tensors, dps):
        self.tensors = tensors
        self.chips = tensors // 2
        self.dps = dps
        self.me = lax.axis_index("tensor")
        self.z = lax.shift_right_logical(self.me, 1)
        self.core = lax.bitwise_and(self.me, 1)
        self.swap_pairs = [(i, i ^ 1) for i in range(tensors)]
        chips = self.chips
        self.moves = []
        for chip in range(chips):
            found = []
            for k in range(1, chips):
                found += [(k, d) for d in (-1, 1) if 0 <= chip + d * k < chips]
            self.moves.append(found)
        table = []
        for device in range(tensors):
            chip, c = divmod(device, 2)
            for k, d in [(0, 0)] + self.moves[chip]:
                owner = chip + d * k
                table += [2 * owner + c, 2 * owner + 1 - c]
        self.table = jnp.array(table, jnp.int32)
        self.scalars = {"even": self.core == 0}
        for chip in range(chips):
            self.scalars["chip%d" % chip] = self.z == chip

    def at(self, chips):
        return functools.reduce(jnp.logical_or, [self.scalars["chip%d" % chip] for chip in chips])

    def sources(self, k, d):
        chips = self.chips
        return [i for i in range(chips) if 0 <= i - d < chips and 0 <= i + d * (k - 1) < chips]

    def flood(self, k, up, down):
        pairs = []
        for d in (1, -1):
            pairs.append([(2 * i + c, 2 * (i - d) + c) for i in self.sources(k, d) for c in range(2)])
        if not set(self.sources(k, 1)) & set(self.sources(k, -1)):
            chosen = jnp.where(self.at(self.sources(k, 1)), up, down)
            both = lax.ppermute(chosen, "tensor", pairs[0] + pairs[1])
            return both, both
        return lax.ppermute(up, "tensor", pairs[0]), lax.ppermute(down, "tensor", pairs[1])

    def piece(self, p, ups, downs):
        chosen = []
        for chip in range(self.chips):
            k, d = self.moves[chip][p - 1]
            block = (ups if d > 0 else downs)[k]
            for entry in chosen:
                if entry[0] is block:
                    entry[1].append(chip)
                    break
            else:
                chosen.append((block, [chip]))
        chosen.sort(key=lambda entry: -len(entry[1]))
        result = chosen[0][0]
        for block, chips in chosen[1:]:
            result = jnp.where(self.at(chips), block, result)
        return result

    def swap(self, x):
        return lax.ppermute(x, "tensor", self.swap_pairs)

    def meet(self, low, high):
        even = self.scalars["even"]
        return jnp.where(even, low, high) + self.swap(jnp.where(even, high, low))

    def order(self, total, other):
        even = self.scalars["even"]
        return jnp.where(even, total, other), jnp.where(even, other, total)

    def part(self, total):
        return self.order(total, self.swap(total))

    def inward(self, i):
        last = self.chips - 1
        pairs = []
        for c in range(2):
            pairs.append((2 * i + c, 2 * (i + 1) + c))
            pairs.append((2 * (last - i) + c, 2 * (last - 1 - i) + c))
        return pairs

    def middle(self):
        left = 2 * (self.chips // 2 - 1)
        pairs = []
        for c in range(2):
            pairs += [(left + c, left + 2 + c), (left + 2 + c, left + c)]
        return pairs

    def low_send(self, step, total, plain):
        inner = self.chips // 2 - 1
        if step < inner:
            mine = packed(total, plain)
            pairs = self.inward(step)
        elif step == inner:
            mine = packed(total, plain)
            pairs = self.middle()
        else:
            mine = total
            pairs = [(to, at) for at, to in self.inward(self.chips - 2 - step)]
        return mine, lax.ppermute(mine, "tensor", pairs)

    def low_take(self, step, total, sent, plain):
        mine, got = sent
        inner = self.chips // 2 - 1
        if step < inner:
            return total + unpacked(got, plain)
        if step == inner:
            return (unpacked(mine, plain) + unpacked(got, plain)).astype(BF)
        i = self.chips - 2 - step
        return jnp.where(self.at([i, self.chips - 1 - i]), got, total)

    def send_across(self, total, k):
        pairs = [(i, i ^ (2 * k)) for i in range(self.tensors)]
        mine = total.astype(BF) if 2 * k == self.chips else total
        return mine, lax.ppermute(mine, "tensor", pairs)

    def dp_bits(self, flip):
        bits = [1 << b for b in range(self.dps.bit_length() - 1)]
        return bits[::-1] if flip else bits

    def dp_send(self, part, bit):
        mine = part.astype(BF)
        return mine, lax.ppermute(mine, "dp", [(i, i ^ bit) for i in range(self.dps)])

    def sum_four(self, part, one, other):
        mine = part.astype(BF)
        gots = []
        for bits in (one ^ other, one, other):
            pairs = [(i, i ^ bits) for i in range(self.dps)]
            gots.append(lax.ppermute(mine, "dp", pairs))
        far, near, side = gots
        return summed([mine, near]) + summed([side, far])


def local(
    tensors,
    dps,
    inputs,
    cotangent,
    gate_pre,
    up_pre,
    down_weight,
    gate_a,
    gate_b,
    up_a,
    up_b,
    down_a,
    down_adapter_second,
):
    places = Places(tensors, dps)
    tokens, width = inputs.shape
    rank = gate_b.shape[0]
    hops = places.chips - 1
    barrier = lax.optimization_barrier

    cut = tokens - tokens // 3
    span_a, span_b = (cut, tokens - cut), (0, cut)
    da = down_a.T
    inputs, me, places.scalars = barrier((inputs, places.me.reshape(1), places.scalars))

    def arrived(hop, block):
        return [(2 * hop + 2, block), (2 * hop + 3, places.swap(block))]

    plain = 2 * rank
    up, down = places.flood(1, cotangent, cotangent)
    low_part = low_call(inputs, gate_a.T, up_a.T, cotangent, down_adapter_second)
    swapped = places.swap(cotangent)
    half = low_part.shape[1] // 2
    low_sum = places.meet(low_part[:, :half], low_part[:, half:])
    down_part, hidden, factor, act = hidden_call(gate_pre, up_pre, da)
    up, down, low_sum, down_part = barrier((up, down, low_sum, down_part))
    ups, downs = [None, up], [None, down]

    def rows_of(blocks, span):
        return [block if block is None else block[span[0] : span[0] + span[1]] for block in blocks]

    sent = places.low_send(0, low_sum, plain)
    pieces = [(0, cotangent), (1, swapped)]
    acc = None
    for hop in range(1, hops):
        last = hop == hops - 1
        if last:
            up, down = places.flood(hop + 1, *(rows_of([x[hop]], span_a)[0] for x in (ups, downs)))
        else:
            up, down = places.flood(hop + 1, ups[hop], downs[hop])
        low_sum = places.low_take(hop - 1, low_sum, sent, plain)
        sent = places.low_send(hop, low_sum, plain)
        acc = grad_call(
            "more", (0, tokens), places.table, me,
            pieces + arrived(hop - 1, places.piece(hop, ups, downs)), down_weight, acc,
        )
        pieces = []
        blocks = [up] if up is down else [up, down]
        if last:
            behind = rows_of(ups, span_b), rows_of(downs, span_b)
            blocks, acc, behind = barrier((blocks, acc, behind))
            acc, sent = barrier((acc, sent))
        else:
            blocks, acc = barrier((blocks, acc))
            acc, sent = barrier((acc, sent))
        up, down = blocks[0], blocks[-1]
        if not last:
            ups.append(up)
            downs.append(down)
    low_sum = places.low_take(hops - 1, low_sum, sent, plain)

    held = places.piece(hops, rows_of(ups, span_a) + [up], rows_of(downs, span_a) + [down])
    ups, downs = behind
    up, _ = places.flood(hops, ups[-1], downs[-1])
    low_all = jnp.concatenate(places.part(low_sum), axis=1)
    low = low_all[: 2 * rank] * BF(adapter_scale_factor)
    back = low_all[2 * rank :]
    rest = [back, da, factor, act, gate_b, up_b, low]
    early = places.dp_send(dot_nn(back, hidden), places.dp_bits(False)[0])
    part_a, second = grad_call(
        "last_a", span_a, places.table, me, arrived(hops - 1, held), down_weight, acc, rest
    )
    up, second, part_a, early = barrier((up, second, part_a, early))
    coming = places.piece(hops, ups + [up], downs + [up])
    rows = down_part.shape[0]
    before = places.meet(
        jnp.concatenate([down_part[: rows // 2], part_a[: span_a[1] // 2]], axis=0),
        jnp.concatenate([down_part[rows // 2 :], part_a[span_a[1] // 2 :]], axis=0),
    )
    before = places.send_across(before, 1)
    early = places.dp_send(summed(early), places.dp_bits(False)[1])
    part_b, *large = grad_call(
        "last_b", span_b, places.table, me, arrived(hops - 1, coming), down_weight, acc,
        rest, second, True,
    )
    part_b, before, early = barrier((part_b, before, early))

    bits = [places.dp_bits(flip) for flip in (False, True)]
    sent = [places.dp_send(x, order[0]) for x, order in zip(large, bits)]
    half = part_b.shape[0] // 2
    after = places.meet(part_b[:half], part_b[half:])
    across = places.send_across(after, 1)
    before = summed(before)
    k = 2
    while k < places.chips:
        beside = places.send_across(before, k)
        sent, across = barrier((sent, across))
        if k == 2:
            large = [summed(pair) for pair in sent]
            sent = [places.dp_send(x, order[1]) for x, order in zip(large, bits)]
        across = places.send_across(summed(across), k)
        beside, across = barrier((beside, across))
        before = summed(beside)
        k *= 2
    total = jnp.concatenate([before, summed(across)], axis=0).astype(BF)
    other, sent = barrier((places.swap(total), sent))
    large = [summed(pair) for pair in sent]
    sums = places.order(total, other)
    down_low = jnp.concatenate([both[: rows // 2] for both in sums], axis=0)
    down_low = jnp.concatenate(
        [down_low[i * rank : (i + 1) * rank] for i in range(tokens // LANES)], axis=1
    )
    ends = (rows // 2, rows // 2 + span_a[1] // 2)
    totals = jnp.concatenate(
        [both[ends[1] :] for both in sums] + [both[ends[0] : ends[1]] for both in sums], axis=0
    )
    firsts = jnp.concatenate([dot_tn(totals, inputs), dot_nn(down_low, cotangent)], axis=0)
    firsts = firsts * adapter_scale_factor
    grad_down_t = summed(early)
    for bit in places.dp_bits(False)[2:]:
        grad_down_t = summed(places.dp_send(grad_down_t, bit))
    for i in range(2, len(bits[0])):
        large = [summed(places.dp_send(x, order[i])) for x, order in zip(large, bits)]
    for i in range(0, len(bits[0]), 2):
        firsts = places.sum_four(firsts, bits[0][i], bits[0][i + 1])
    gate_second, up_second = large
    gate_first = firsts[:rank]
    up_first = firsts[rank : 2 * rank]
    down_second = firsts[2 * rank :]
    return (gate_first.T, gate_second, up_first.T, up_second, grad_down_t.T, down_second)


def solution(mesh):
    placed = (
        P("dp", "tensor"),
        P("dp", "tensor"),
        P("dp", "tensor"),
        P("dp", "tensor"),
        P("tensor", None),
        P("tensor", None),
        P(None, "tensor"),
        P("tensor", None),
        P(None, "tensor"),
        P("tensor", None),
        P(None, "tensor"),
    )
    return jax.shard_map(
        functools.partial(local, mesh.shape["tensor"], mesh.shape["dp"]),
        mesh=mesh,
        in_specs=placed,
        out_specs=(
            P("tensor", None),
            P(None, "tensor"),
            P("tensor", None),
            P(None, "tensor"),
            P("tensor", None),
            P(None, "tensor"),
        ),
        check_vma=False,
    )
```

```python
import functools

import jax
import jax.numpy as jnp
from jax import lax
from jax.experimental import pallas as pl
from jax.experimental.pallas import tpu as pltpu
from jax.sharding import PartitionSpec as P

adapter_scale_factor = 2.0
LANES = 128
BF = jnp.bfloat16
F32 = jnp.float32


def silu_parts(pre):
    sigma = 0.5 + 0.5 * jnp.tanh(0.5 * pre)
    return pre * sigma, sigma * (1.0 + pre * (1.0 - sigma))


def dot_nt(left, right):
    return lax.dot_general(left, right, (((1,), (1,)), ((), ())), preferred_element_type=F32)


def dot_nn(left, right):
    return jnp.dot(left, right, preferred_element_type=F32)


def dot_tn(left, right):
    return lax.dot_general(left, right, (((0,), (0,)), ((), ())), preferred_element_type=F32)


def pin(x, *after):
    return lax.optimization_barrier((x, *after))[0]


def divisor(size, most):
    best = LANES
    for width in range(LANES, most + 1, LANES):
        if size % width == 0:
            best = width
    return best


def cost(flops, moved, transcendentals=0):
    return pl.CostEstimate(flops=flops, bytes_accessed=moved, transcendentals=transcendentals)


def grad_kernel(n_blocks, has_acc, finish, first, final, *refs):
    blocks = refs[2 : 2 + n_blocks]
    weights = refs[2 + n_blocks : 2 + 2 * n_blocks]
    refs = refs[2 + 2 * n_blocks :]
    grad = dot_nt(blocks[0][...], weights[0][...])
    for block, w_ref in zip(blocks[1:], weights[1:]):
        grad = grad + dot_nt(block[...], w_ref[...])
    if has_acc:
        grad = grad + refs[0][...]
        refs = refs[1:]
    if not finish:
        refs[0][...] = grad
        return
    back_ref, da_ref, factor_ref, act_ref, gb_ref, ub_ref, low_ref = refs[:7]
    part_ref = refs[-3 if final else -2]
    step = pl.program_id(0)
    grad = grad + dot_tn(back_ref[...], da_ref[...])
    gate_grad = (grad * factor_ref[...]).astype(BF)
    up_grad = (grad * act_ref[...]).astype(BF)
    zeros = jnp.zeros_like(gb_ref)
    part = dot_nt(gate_grad, jnp.concatenate([gb_ref[...], zeros], axis=0))
    part = part + dot_nt(up_grad, jnp.concatenate([zeros, ub_ref[...]], axis=0))

    @pl.when(step == 0)
    def _():
        part_ref[...] = part

    @pl.when(step > 0)
    def _():
        part_ref[...] += part

    rank = low_ref.shape[0] // 2
    gate_second = dot_nn(low_ref[:rank, :], gate_grad)
    up_second = dot_nn(low_ref[rank:, :], up_grad)
    if not first:
        gate_second = refs[7][:rank, :] + gate_second
        up_second = refs[7][rank:, :] + up_second
    if final:
        refs[-2][...] = gate_second.astype(BF)
        refs[-1][...] = up_second.astype(BF)
    else:
        refs[-1][:rank, :] = gate_second
        refs[-1][rank:, :] = up_second


def grad_call(name, span, table, me, pieces, weight, acc, rest=None, second=None, final=False):
    at, size = span
    index = at // size
    hidden = weight.shape[0]
    blocks = [block for _, block in pieces]
    width = blocks[0].shape[1]
    tile = divisor(hidden, 768)
    finish = rest is not None
    per = int(round(table.shape[0] ** 0.5))
    in_specs = [pl.BlockSpec((size, width), lambda j, t, m: (0, 0)) for _ in blocks]
    for column, _ in pieces:
        in_specs.append(
            pl.BlockSpec(
                (tile, width), lambda j, t, m, column=column: (j, t[m[0] * per + column])
            )
        )
    args = [*blocks, *[weight] * len(blocks)]
    if acc is not None:
        in_specs.append(pl.BlockSpec((size, tile), lambda j, t, m: (index, j)))
        args.append(acc)
    flops = 2 * size * hidden * width * len(blocks)
    moved = 2 * hidden * width * len(blocks) + 8 * size * hidden
    if finish:
        back, low = rest[0], rest[-1]
        ranks = low.shape[0]
        rank = ranks // 2
        flops += 2 * size * hidden * 8 * ranks
        in_specs += [
            pl.BlockSpec((rank, size), lambda j, t, m: (0, index)),
            pl.BlockSpec((rank, tile), lambda j, t, m: (0, j)),
            pl.BlockSpec((size, tile), lambda j, t, m: (index, j)),
            pl.BlockSpec((size, tile), lambda j, t, m: (index, j)),
            pl.BlockSpec((rank, tile), lambda j, t, m: (0, j)),
            pl.BlockSpec((rank, tile), lambda j, t, m: (0, j)),
            pl.BlockSpec((ranks, size), lambda j, t, m: (0, index)),
        ]
        args += rest
        if second is not None:
            in_specs.append(pl.BlockSpec((ranks, tile), lambda j, t, m: (0, j)))
            args.append(second)
        out_specs = [pl.BlockSpec((size, ranks), lambda j, t, m: (0, 0))]
        out_shape = [jax.ShapeDtypeStruct((size, ranks), F32)]
        if final:
            out_specs += [pl.BlockSpec((rank, tile), lambda j, t, m: (0, j))] * 2
            out_shape += [jax.ShapeDtypeStruct((rank, hidden), BF)] * 2
        else:
            out_specs.append(pl.BlockSpec((ranks, tile), lambda j, t, m: (0, j)))
            out_shape.append(jax.ShapeDtypeStruct((ranks, hidden), F32))
    else:
        out_specs = pl.BlockSpec((size, tile), lambda j, t, m: (0, j))
        out_shape = jax.ShapeDtypeStruct((size, hidden), F32)
    return pl.pallas_call(
        functools.partial(
            grad_kernel, len(blocks), acc is not None, finish, second is None, final
        ),
        grid_spec=pltpu.PrefetchScalarGridSpec(
            num_scalar_prefetch=2,
            grid=(hidden // tile,),
            in_specs=in_specs,
            out_specs=out_specs,
        ),
        out_shape=out_shape,
        compiler_params=pltpu.CompilerParams(vmem_limit_bytes=36 * 1024 * 1024),
        cost_estimate=cost(flops, moved),
        name=name,
    )(table, me, *args)


def low_kernel(x_ref, ga_ref, ua_ref, cot_ref, s_ref, low_ref):
    rank = s_ref.shape[0]
    both = jnp.concatenate([ga_ref[...], ua_ref[...]], axis=0)
    low_ref[: 2 * rank, :] = dot_nt(x_ref[...], both).T
    back = adapter_scale_factor * dot_nt(cot_ref[...], s_ref[...])
    low_ref[2 * rank :, :] = back.T


def low_call(inputs, ga, ua, cotangent, second):
    return pl.pallas_call(
        low_kernel,
        out_shape=jax.ShapeDtypeStruct((3 * second.shape[0], inputs.shape[0]), F32),
        compiler_params=pltpu.CompilerParams(vmem_limit_bytes=60 * 1024 * 1024),
        cost_estimate=cost(1024, 1024),
        name="low",
    )(inputs, ga, ua, cotangent, second)


def hidden_kernel(gate_ref, up_ref, da_ref, down_ref, hidden_ref, factor_ref, act_ref, acc_ref):
    step = pl.program_id(0)
    up = up_ref[...].astype(F32)
    act, slope = silu_parts(gate_ref[...].astype(F32))
    factor_ref[...] = up * slope
    act_ref[...] = act
    hidden = (act * up).astype(BF)
    hidden_ref[...] = hidden
    part = dot_nt(hidden, da_ref[...])

    @pl.when(step == 0)
    def _():
        acc_ref[...] = part

    @pl.when(step > 0)
    def _():
        acc_ref[...] += part

    @pl.when(step == pl.num_programs(0) - 1)
    def _():
        turned = acc_ref[...].T
        rank = turned.shape[0]
        for i in range(turned.shape[1] // LANES):
            down_ref[i * rank : (i + 1) * rank, :] = turned[:, i * LANES : (i + 1) * LANES]


def hidden_call(gate_pre, up_pre, da):
    tokens, hidden = gate_pre.shape
    rank = da.shape[0]
    tile = divisor(hidden, 384)
    rows = rank * tokens // LANES
    wide = pl.BlockSpec((tokens, tile), lambda j: (0, j))
    return pl.pallas_call(
        hidden_kernel,
        grid=(hidden // tile,),
        in_specs=[wide, wide, pl.BlockSpec((rank, tile), lambda j: (0, j))],
        out_specs=[pl.BlockSpec((rows, LANES), lambda j: (0, 0)), wide, wide, wide],
        out_shape=[
            jax.ShapeDtypeStruct((rows, LANES), F32),
            jax.ShapeDtypeStruct((tokens, hidden), BF),
            jax.ShapeDtypeStruct((tokens, hidden), F32),
            jax.ShapeDtypeStruct((tokens, hidden), F32),
        ],
        scratch_shapes=[pltpu.VMEM((tokens, rank), F32)],
        compiler_params=pltpu.CompilerParams(vmem_limit_bytes=60 * 1024 * 1024),
        cost_estimate=cost(1024, 1024),
        name="hidden",
    )(gate_pre, up_pre, da)


def packed(x, plain):
    upper = lax.reduce_precision(x[plain:], exponent_bits=8, mantissa_bits=7)
    rest = x[plain:] - upper
    return jnp.concatenate([x[:plain], upper, rest], axis=0).astype(BF)


def unpacked(x, plain):
    x = x.astype(F32)
    end = (plain + x.shape[0]) // 2
    return jnp.concatenate([x[:plain], x[plain:end] + x[end:]], axis=0)


def summed(values):
    total = values[0].astype(F32)
    for value in values[1:]:
        total = total + value.astype(F32)
    return total


class Places:
    def __init__(self, tensors, dps):
        self.tensors = tensors
        self.chips = tensors // 2
        self.dps = dps
        self.me = lax.axis_index("tensor")
        self.z = lax.shift_right_logical(self.me, 1)
        self.core = lax.bitwise_and(self.me, 1)
        self.swap_pairs = [(i, i ^ 1) for i in range(tensors)]
        chips = self.chips
        self.moves = []
        for chip in range(chips):
            found = []
            for k in range(1, chips):
                found += [(k, d) for d in (-1, 1) if 0 <= chip + d * k < chips]
            self.moves.append(found)
        table = []
        for device in range(tensors):
            chip, c = divmod(device, 2)
            for k, d in [(0, 0)] + self.moves[chip]:
                owner = chip + d * k
                table += [2 * owner + c, 2 * owner + 1 - c]
        self.table = jnp.array(table, jnp.int32)
        self.scalars = {"even": self.core == 0}
        for chip in range(chips):
            self.scalars["chip%d" % chip] = self.z == chip

    def at(self, chips):
        return functools.reduce(jnp.logical_or, [self.scalars["chip%d" % chip] for chip in chips])

    def sources(self, k, d):
        chips = self.chips
        return [i for i in range(chips) if 0 <= i - d < chips and 0 <= i + d * (k - 1) < chips]

    def flood(self, k, up, down):
        pairs = []
        for d in (1, -1):
            pairs.append([(2 * i + c, 2 * (i - d) + c) for i in self.sources(k, d) for c in range(2)])
        if not set(self.sources(k, 1)) & set(self.sources(k, -1)):
            chosen = jnp.where(self.at(self.sources(k, 1)), up, down)
            both = lax.ppermute(chosen, "tensor", pairs[0] + pairs[1])
            return both, both
        return lax.ppermute(up, "tensor", pairs[0]), lax.ppermute(down, "tensor", pairs[1])

    def piece(self, p, ups, downs):
        chosen = []
        for chip in range(self.chips):
            k, d = self.moves[chip][p - 1]
            block = (ups if d > 0 else downs)[k]
            for entry in chosen:
                if entry[0] is block:
                    entry[1].append(chip)
                    break
            else:
                chosen.append((block, [chip]))
        chosen.sort(key=lambda entry: -len(entry[1]))
        result = chosen[0][0]
        for block, chips in chosen[1:]:
            result = jnp.where(self.at(chips), block, result)
        return result

    def swap(self, x):
        return lax.ppermute(x, "tensor", self.swap_pairs)

    def meet(self, low, high):
        even = self.scalars["even"]
        return jnp.where(even, low, high) + self.swap(jnp.where(even, high, low))

    def order(self, total, other):
        even = self.scalars["even"]
        return jnp.where(even, total, other), jnp.where(even, other, total)

    def part(self, total):
        return self.order(total, self.swap(total))

    def inward(self, i):
        last = self.chips - 1
        pairs = []
        for c in range(2):
            pairs.append((2 * i + c, 2 * (i + 1) + c))
            pairs.append((2 * (last - i) + c, 2 * (last - 1 - i) + c))
        return pairs

    def middle(self):
        left = 2 * (self.chips // 2 - 1)
        pairs = []
        for c in range(2):
            pairs += [(left + c, left + 2 + c), (left + 2 + c, left + c)]
        return pairs

    def low_send(self, step, total, plain):
        inner = self.chips // 2 - 1
        if step < inner:
            mine = packed(total, plain)
            pairs = self.inward(step)
        elif step == inner:
            mine = packed(total, plain)
            pairs = self.middle()
        else:
            mine = total
            pairs = [(to, at) for at, to in self.inward(self.chips - 2 - step)]
        return mine, lax.ppermute(mine, "tensor", pairs)

    def low_take(self, step, total, sent, plain):
        mine, got = sent
        inner = self.chips // 2 - 1
        if step < inner:
            return total + unpacked(got, plain)
        if step == inner:
            return (unpacked(mine, plain) + unpacked(got, plain)).astype(BF)
        i = self.chips - 2 - step
        return jnp.where(self.at([i, self.chips - 1 - i]), got, total)

    def send_across(self, total, k):
        pairs = [(i, i ^ (2 * k)) for i in range(self.tensors)]
        mine = total.astype(BF) if 2 * k == self.chips else total
        return mine, lax.ppermute(mine, "tensor", pairs)

    def dp_bits(self, flip):
        bits = [1 << b for b in range(self.dps.bit_length() - 1)]
        return bits[::-1] if flip else bits

    def dp_send(self, part, bit):
        mine = part.astype(BF)
        return mine, lax.ppermute(mine, "dp", [(i, i ^ bit) for i in range(self.dps)])

    def sum_four(self, part, one, other):
        mine = part.astype(BF)
        gots = []
        for bits in (one ^ other, one, other):
            pairs = [(i, i ^ bits) for i in range(self.dps)]
            gots.append(lax.ppermute(mine, "dp", pairs))
        far, near, side = gots
        return summed([mine, near]) + summed([side, far])


def local(
    tensors,
    dps,
    inputs,
    cotangent,
    gate_pre,
    up_pre,
    down_weight,
    gate_a,
    gate_b,
    up_a,
    up_b,
    down_a,
    down_adapter_second,
):
    places = Places(tensors, dps)
    tokens, width = inputs.shape
    rank = gate_b.shape[0]
    hops = places.chips - 1
    barrier = lax.optimization_barrier

    cut = tokens - tokens // 3
    span_a, span_b = (cut, tokens - cut), (0, cut)
    da = down_a.T
    inputs, me, places.scalars = barrier((inputs, places.me.reshape(1), places.scalars))

    def arrived(hop, block):
        return [(2 * hop + 2, block), (2 * hop + 3, places.swap(block))]

    plain = 2 * rank
    up, down = places.flood(1, cotangent, cotangent)
    low_part = low_call(inputs, gate_a.T, up_a.T, cotangent, down_adapter_second)
    swapped = places.swap(cotangent)
    half = low_part.shape[1] // 2
    low_sum = places.meet(low_part[:, :half], low_part[:, half:])
    down_part, hidden, factor, act = hidden_call(gate_pre, up_pre, da)
    up, down, low_sum, down_part = barrier((up, down, low_sum, down_part))
    ups, downs = [None, up], [None, down]

    def rows_of(blocks, span):
        return [block if block is None else block[span[0] : span[0] + span[1]] for block in blocks]

    sent = places.low_send(0, low_sum, plain)
    pieces = [(0, cotangent), (1, swapped)]
    acc = None
    for hop in range(1, hops):
        last = hop == hops - 1
        if last:
            up, down = places.flood(hop + 1, *(rows_of([x[hop]], span_a)[0] for x in (ups, downs)))
        else:
            up, down = places.flood(hop + 1, ups[hop], downs[hop])
        low_sum = places.low_take(hop - 1, low_sum, sent, plain)
        sent = places.low_send(hop, low_sum, plain)
        acc = grad_call(
            "more", (0, tokens), places.table, me,
            pieces + arrived(hop - 1, places.piece(hop, ups, downs)), down_weight, acc,
        )
        pieces = []
        blocks = [up] if up is down else [up, down]
        if last:
            behind = rows_of(ups, span_b), rows_of(downs, span_b)
            blocks, acc, behind = barrier((blocks, acc, behind))
            acc, sent = barrier((acc, sent))
        else:
            blocks, acc = barrier((blocks, acc))
            acc, sent = barrier((acc, sent))
        up, down = blocks[0], blocks[-1]
        if not last:
            ups.append(up)
            downs.append(down)
    low_sum = places.low_take(hops - 1, low_sum, sent, plain)

    held = places.piece(hops, rows_of(ups, span_a) + [up], rows_of(downs, span_a) + [down])
    ups, downs = behind
    up, _ = places.flood(hops, ups[-1], downs[-1])
    low_all = jnp.concatenate(places.part(low_sum), axis=1)
    low = low_all[: 2 * rank] * BF(adapter_scale_factor)
    back = low_all[2 * rank :]
    rest = [back, da, factor, act, gate_b, up_b, low]
    early = places.dp_send(dot_nn(back, hidden), places.dp_bits(False)[0])
    part_a, second = grad_call(
        "last_a", span_a, places.table, me, arrived(hops - 1, held), down_weight, acc, rest
    )
    up, second, part_a, early = barrier((up, second, part_a, early))
    coming = places.piece(hops, ups + [up], downs + [up])
    rows = down_part.shape[0]
    before = places.meet(
        jnp.concatenate([down_part[: rows // 2], part_a[: span_a[1] // 2]], axis=0),
        jnp.concatenate([down_part[rows // 2 :], part_a[span_a[1] // 2 :]], axis=0),
    )
    before = places.send_across(before, 1)
    early = places.dp_send(summed(early), places.dp_bits(False)[1])
    part_b, *large = grad_call(
        "last_b", span_b, places.table, me, arrived(hops - 1, coming), down_weight, acc,
        rest, second, True,
    )
    part_b, before, early = barrier((part_b, before, early))

    bits = [places.dp_bits(flip) for flip in (False, True)]
    sent = [places.dp_send(x, order[0]) for x, order in zip(large, bits)]
    half = part_b.shape[0] // 2
    after = places.meet(part_b[:half], part_b[half:])
    across = places.send_across(after, 1)
    k = 2
    while k < places.chips:
        before, across = barrier((before, across))
        before = places.send_across(summed(before), k)
        across = places.send_across(summed(across), k)
        k *= 2
    large = [summed(pair) for pair in sent]
    sent = [places.dp_send(x, order[1]) for x, order in zip(large, bits)]
    total = jnp.concatenate([summed(before), summed(across)], axis=0).astype(BF)
    other, sent = barrier((places.swap(total), sent))
    large = [summed(pair) for pair in sent]
    sums = places.order(total, other)
    down_low = jnp.concatenate([both[: rows // 2] for both in sums], axis=0)
    down_low = jnp.concatenate(
        [down_low[i * rank : (i + 1) * rank] for i in range(tokens // LANES)], axis=1
    )
    ends = (rows // 2, rows // 2 + span_a[1] // 2)
    totals = jnp.concatenate(
        [both[ends[1] :] for both in sums] + [both[ends[0] : ends[1]] for both in sums], axis=0
    )
    firsts = jnp.concatenate([dot_tn(totals, inputs), dot_nn(down_low, cotangent)], axis=0)
    firsts = firsts * adapter_scale_factor
    grad_down_t = summed(early)
    for bit in places.dp_bits(False)[2:]:
        grad_down_t = summed(places.dp_send(grad_down_t, bit))
    for i in range(2, len(bits[0])):
        large = [summed(places.dp_send(x, order[i])) for x, order in zip(large, bits)]
    for i in range(0, len(bits[0]), 2):
        firsts = places.sum_four(firsts, bits[0][i], bits[0][i + 1])
    gate_second, up_second = large
    gate_first = firsts[:rank]
    up_first = firsts[rank : 2 * rank]
    down_second = firsts[2 * rank :]
    return (gate_first.T, gate_second, up_first.T, up_second, grad_down_t.T, down_second)


def solution(mesh):
    placed = (
        P("dp", "tensor"),
        P("dp", "tensor"),
        P("dp", "tensor"),
        P("dp", "tensor"),
        P("tensor", None),
        P("tensor", None),
        P(None, "tensor"),
        P("tensor", None),
        P(None, "tensor"),
        P("tensor", None),
        P(None, "tensor"),
    )
    return jax.shard_map(
        functools.partial(local, mesh.shape["tensor"], mesh.shape["dp"]),
        mesh=mesh,
        in_specs=placed,
        out_specs=(
            P("tensor", None),
            P(None, "tensor"),
            P("tensor", None),
            P(None, "tensor"),
            P("tensor", None),
            P(None, "tensor"),
        ),
        check_vma=False,
    )
```

```python
import functools

import jax
import jax.numpy as jnp
from jax import lax
from jax.experimental import pallas as pl
from jax.experimental.pallas import tpu as pltpu
from jax.sharding import PartitionSpec as P

adapter_scale_factor = 2.0
LANES = 128
BF = jnp.bfloat16
F32 = jnp.float32


def silu_parts(pre):
    sigma = 0.5 + 0.5 * jnp.tanh(0.5 * pre)
    return pre * sigma, sigma * (1.0 + pre * (1.0 - sigma))


def dot_nt(left, right):
    return lax.dot_general(left, right, (((1,), (1,)), ((), ())), preferred_element_type=F32)


def dot_nn(left, right):
    return jnp.dot(left, right, preferred_element_type=F32)


def dot_tn(left, right):
    return lax.dot_general(left, right, (((0,), (0,)), ((), ())), preferred_element_type=F32)


def pin(x, *after):
    return lax.optimization_barrier((x, *after))[0]


def divisor(size, most):
    best = LANES
    for width in range(LANES, most + 1, LANES):
        if size % width == 0:
            best = width
    return best


def cost(flops, moved, transcendentals=0):
    return pl.CostEstimate(flops=flops, bytes_accessed=moved, transcendentals=transcendentals)


def grad_kernel(n_blocks, has_acc, finish, first, final, *refs):
    blocks = refs[2 : 2 + n_blocks]
    weights = refs[2 + n_blocks : 2 + 2 * n_blocks]
    refs = refs[2 + 2 * n_blocks :]
    grad = dot_nt(blocks[0][...], weights[0][...])
    for block, w_ref in zip(blocks[1:], weights[1:]):
        grad = grad + dot_nt(block[...], w_ref[...])
    if has_acc:
        grad = grad + refs[0][...]
        refs = refs[1:]
    if not finish:
        refs[0][...] = grad
        return
    back_ref, da_ref, factor_ref, act_ref, gb_ref, ub_ref, low_ref = refs[:7]
    part_ref = refs[-3 if final else -2]
    step = pl.program_id(0)
    grad = grad + dot_tn(back_ref[...], da_ref[...])
    gate_grad = (grad * factor_ref[...]).astype(BF)
    up_grad = (grad * act_ref[...]).astype(BF)
    zeros = jnp.zeros_like(gb_ref)
    part = dot_nt(gate_grad, jnp.concatenate([gb_ref[...], zeros], axis=0))
    part = part + dot_nt(up_grad, jnp.concatenate([zeros, ub_ref[...]], axis=0))

    @pl.when(step == 0)
    def _():
        part_ref[...] = part

    @pl.when(step > 0)
    def _():
        part_ref[...] += part

    rank = low_ref.shape[0] // 2
    gate_second = dot_nn(low_ref[:rank, :], gate_grad)
    up_second = dot_nn(low_ref[rank:, :], up_grad)
    if not first:
        gate_second = refs[7][:rank, :] + gate_second
        up_second = refs[7][rank:, :] + up_second
    if final:
        refs[-2][...] = gate_second.astype(BF)
        refs[-1][...] = up_second.astype(BF)
    else:
        refs[-1][:rank, :] = gate_second
        refs[-1][rank:, :] = up_second


def grad_call(name, span, table, me, pieces, weight, acc, rest=None, second=None, final=False):
    at, size = span
    index = at // size
    hidden = weight.shape[0]
    blocks = [block for _, block in pieces]
    width = blocks[0].shape[1]
    tile = divisor(hidden, 768)
    finish = rest is not None
    per = int(round(table.shape[0] ** 0.5))
    in_specs = [pl.BlockSpec((size, width), lambda j, t, m: (0, 0)) for _ in blocks]
    for column, _ in pieces:
        in_specs.append(
            pl.BlockSpec(
                (tile, width), lambda j, t, m, column=column: (j, t[m[0] * per + column])
            )
        )
    args = [*blocks, *[weight] * len(blocks)]
    if acc is not None:
        in_specs.append(pl.BlockSpec((size, tile), lambda j, t, m: (index, j)))
        args.append(acc)
    flops = 2 * size * hidden * width * len(blocks)
    moved = 2 * hidden * width * len(blocks) + 8 * size * hidden
    if finish:
        back, low = rest[0], rest[-1]
        ranks = low.shape[0]
        rank = ranks // 2
        flops += 2 * size * hidden * 8 * ranks
        in_specs += [
            pl.BlockSpec((rank, size), lambda j, t, m: (0, index)),
            pl.BlockSpec((rank, tile), lambda j, t, m: (0, j)),
            pl.BlockSpec((size, tile), lambda j, t, m: (index, j)),
            pl.BlockSpec((size, tile), lambda j, t, m: (index, j)),
            pl.BlockSpec((rank, tile), lambda j, t, m: (0, j)),
            pl.BlockSpec((rank, tile), lambda j, t, m: (0, j)),
            pl.BlockSpec((ranks, size), lambda j, t, m: (0, index)),
        ]
        args += rest
        if second is not None:
            in_specs.append(pl.BlockSpec((ranks, tile), lambda j, t, m: (0, j)))
            args.append(second)
        out_specs = [pl.BlockSpec((size, ranks), lambda j, t, m: (0, 0))]
        out_shape = [jax.ShapeDtypeStruct((size, ranks), F32)]
        if final:
            out_specs += [pl.BlockSpec((rank, tile), lambda j, t, m: (0, j))] * 2
            out_shape += [jax.ShapeDtypeStruct((rank, hidden), BF)] * 2
        else:
            out_specs.append(pl.BlockSpec((ranks, tile), lambda j, t, m: (0, j)))
            out_shape.append(jax.ShapeDtypeStruct((ranks, hidden), F32))
    else:
        out_specs = pl.BlockSpec((size, tile), lambda j, t, m: (0, j))
        out_shape = jax.ShapeDtypeStruct((size, hidden), F32)
    return pl.pallas_call(
        functools.partial(
            grad_kernel, len(blocks), acc is not None, finish, second is None, final
        ),
        grid_spec=pltpu.PrefetchScalarGridSpec(
            num_scalar_prefetch=2,
            grid=(hidden // tile,),
            in_specs=in_specs,
            out_specs=out_specs,
        ),
        out_shape=out_shape,
        compiler_params=pltpu.CompilerParams(vmem_limit_bytes=36 * 1024 * 1024),
        cost_estimate=cost(flops, moved),
        name=name,
    )(table, me, *args)


def low_kernel(x_ref, ga_ref, ua_ref, cot_ref, s_ref, low_ref):
    rank = s_ref.shape[0]
    both = jnp.concatenate([ga_ref[...], ua_ref[...]], axis=0)
    low_ref[: 2 * rank, :] = dot_nt(x_ref[...], both).T
    back = adapter_scale_factor * dot_nt(cot_ref[...], s_ref[...])
    low_ref[2 * rank :, :] = back.T


def low_call(inputs, ga, ua, cotangent, second):
    return pl.pallas_call(
        low_kernel,
        out_shape=jax.ShapeDtypeStruct((3 * second.shape[0], inputs.shape[0]), F32),
        compiler_params=pltpu.CompilerParams(vmem_limit_bytes=60 * 1024 * 1024),
        cost_estimate=cost(1024, 1024),
        name="low",
    )(inputs, ga, ua, cotangent, second)


def hidden_kernel(gate_ref, up_ref, da_ref, down_ref, hidden_ref, factor_ref, act_ref, acc_ref):
    step = pl.program_id(0)
    up = up_ref[...].astype(F32)
    act, slope = silu_parts(gate_ref[...].astype(F32))
    factor_ref[...] = up * slope
    act_ref[...] = act
    hidden = (act * up).astype(BF)
    hidden_ref[...] = hidden
    part = dot_nt(hidden, da_ref[...])

    @pl.when(step == 0)
    def _():
        acc_ref[...] = part

    @pl.when(step > 0)
    def _():
        acc_ref[...] += part

    @pl.when(step == pl.num_programs(0) - 1)
    def _():
        turned = acc_ref[...].T
        rank = turned.shape[0]
        for i in range(turned.shape[1] // LANES):
            down_ref[i * rank : (i + 1) * rank, :] = turned[:, i * LANES : (i + 1) * LANES]


def hidden_call(gate_pre, up_pre, da):
    tokens, hidden = gate_pre.shape
    rank = da.shape[0]
    tile = divisor(hidden, 384)
    rows = rank * tokens // LANES
    wide = pl.BlockSpec((tokens, tile), lambda j: (0, j))
    return pl.pallas_call(
        hidden_kernel,
        grid=(hidden // tile,),
        in_specs=[wide, wide, pl.BlockSpec((rank, tile), lambda j: (0, j))],
        out_specs=[pl.BlockSpec((rows, LANES), lambda j: (0, 0)), wide, wide, wide],
        out_shape=[
            jax.ShapeDtypeStruct((rows, LANES), F32),
            jax.ShapeDtypeStruct((tokens, hidden), BF),
            jax.ShapeDtypeStruct((tokens, hidden), F32),
            jax.ShapeDtypeStruct((tokens, hidden), F32),
        ],
        scratch_shapes=[pltpu.VMEM((tokens, rank), F32)],
        compiler_params=pltpu.CompilerParams(vmem_limit_bytes=60 * 1024 * 1024),
        cost_estimate=cost(1024, 1024),
        name="hidden",
    )(gate_pre, up_pre, da)


def packed(x, plain):
    upper = lax.reduce_precision(x[plain:], exponent_bits=8, mantissa_bits=7)
    rest = x[plain:] - upper
    return jnp.concatenate([x[:plain], upper, rest], axis=0).astype(BF)


def unpacked(x, plain):
    x = x.astype(F32)
    end = (plain + x.shape[0]) // 2
    return jnp.concatenate([x[:plain], x[plain:end] + x[end:]], axis=0)


def summed(values):
    total = values[0].astype(F32)
    for value in values[1:]:
        total = total + value.astype(F32)
    return total


class Places:
    def __init__(self, tensors, dps):
        self.tensors = tensors
        self.chips = tensors // 2
        self.dps = dps
        self.me = lax.axis_index("tensor")
        self.z = lax.shift_right_logical(self.me, 1)
        self.core = lax.bitwise_and(self.me, 1)
        self.swap_pairs = [(i, i ^ 1) for i in range(tensors)]
        chips = self.chips
        self.moves = []
        for chip in range(chips):
            found = []
            for k in range(1, chips):
                found += [(k, d) for d in (-1, 1) if 0 <= chip + d * k < chips]
            self.moves.append(found)
        table = []
        for device in range(tensors):
            chip, c = divmod(device, 2)
            for k, d in [(0, 0)] + self.moves[chip]:
                owner = chip + d * k
                table += [2 * owner + c, 2 * owner + 1 - c]
        self.table = jnp.array(table, jnp.int32)
        self.scalars = {"even": self.core == 0}
        for chip in range(chips):
            self.scalars["chip%d" % chip] = self.z == chip

    def at(self, chips):
        return functools.reduce(jnp.logical_or, [self.scalars["chip%d" % chip] for chip in chips])

    def sources(self, k, d):
        chips = self.chips
        return [i for i in range(chips) if 0 <= i - d < chips and 0 <= i + d * (k - 1) < chips]

    def flood(self, k, up, down):
        pairs = []
        for d in (1, -1):
            pairs.append([(2 * i + c, 2 * (i - d) + c) for i in self.sources(k, d) for c in range(2)])
        if not set(self.sources(k, 1)) & set(self.sources(k, -1)):
            chosen = jnp.where(self.at(self.sources(k, 1)), up, down)
            both = lax.ppermute(chosen, "tensor", pairs[0] + pairs[1])
            return both, both
        return lax.ppermute(up, "tensor", pairs[0]), lax.ppermute(down, "tensor", pairs[1])

    def piece(self, p, ups, downs):
        chosen = []
        for chip in range(self.chips):
            k, d = self.moves[chip][p - 1]
            block = (ups if d > 0 else downs)[k]
            for entry in chosen:
                if entry[0] is block:
                    entry[1].append(chip)
                    break
            else:
                chosen.append((block, [chip]))
        chosen.sort(key=lambda entry: -len(entry[1]))
        result = chosen[0][0]
        for block, chips in chosen[1:]:
            result = jnp.where(self.at(chips), block, result)
        return result

    def swap(self, x):
        return lax.ppermute(x, "tensor", self.swap_pairs)

    def meet(self, low, high):
        even = self.scalars["even"]
        return jnp.where(even, low, high) + self.swap(jnp.where(even, high, low))

    def order(self, total, other):
        even = self.scalars["even"]
        return jnp.where(even, total, other), jnp.where(even, other, total)

    def part(self, total):
        return self.order(total, self.swap(total))

    def inward(self, i):
        last = self.chips - 1
        pairs = []
        for c in range(2):
            pairs.append((2 * i + c, 2 * (i + 1) + c))
            pairs.append((2 * (last - i) + c, 2 * (last - 1 - i) + c))
        return pairs

    def middle(self):
        left = 2 * (self.chips // 2 - 1)
        pairs = []
        for c in range(2):
            pairs += [(left + c, left + 2 + c), (left + 2 + c, left + c)]
        return pairs

    def low_send(self, step, total, plain):
        inner = self.chips // 2 - 1
        if step < inner:
            mine = packed(total, plain)
            pairs = self.inward(step)
        elif step == inner:
            mine = packed(total, plain)
            pairs = self.middle()
        else:
            mine = total
            pairs = [(to, at) for at, to in self.inward(self.chips - 2 - step)]
        return mine, lax.ppermute(mine, "tensor", pairs)

    def low_take(self, step, total, sent, plain):
        mine, got = sent
        inner = self.chips // 2 - 1
        if step < inner:
            return total + unpacked(got, plain)
        if step == inner:
            return (unpacked(mine, plain) + unpacked(got, plain)).astype(BF)
        i = self.chips - 2 - step
        return jnp.where(self.at([i, self.chips - 1 - i]), got, total)

    def send_across(self, total, k):
        pairs = [(i, i ^ (2 * k)) for i in range(self.tensors)]
        mine = total.astype(BF) if 2 * k == self.chips else total
        return mine, lax.ppermute(mine, "tensor", pairs)

    def dp_bits(self, flip):
        bits = [1 << b for b in range(self.dps.bit_length() - 1)]
        return bits[::-1] if flip else bits

    def dp_send(self, part, bit):
        mine = part.astype(BF)
        return mine, lax.ppermute(mine, "dp", [(i, i ^ bit) for i in range(self.dps)])

    def sum_four(self, part, one, other):
        mine = part.astype(BF)
        gots = []
        for bits in (one ^ other, one, other):
            pairs = [(i, i ^ bits) for i in range(self.dps)]
            gots.append(lax.ppermute(mine, "dp", pairs))
        far, near, side = gots
        return summed([mine, near]) + summed([side, far])


def local(
    tensors,
    dps,
    inputs,
    cotangent,
    gate_pre,
    up_pre,
    down_weight,
    gate_a,
    gate_b,
    up_a,
    up_b,
    down_a,
    down_adapter_second,
):
    places = Places(tensors, dps)
    tokens, width = inputs.shape
    rank = gate_b.shape[0]
    hops = places.chips - 1
    barrier = lax.optimization_barrier

    cut = tokens - tokens // 3
    span_a, span_b = (cut, tokens - cut), (0, cut)
    da = down_a.T
    inputs, me, places.scalars = barrier((inputs, places.me.reshape(1), places.scalars))

    def arrived(hop, block):
        return [(2 * hop + 2, block), (2 * hop + 3, places.swap(block))]

    plain = 2 * rank
    up, down = places.flood(1, cotangent, cotangent)
    low_part = low_call(inputs, gate_a.T, up_a.T, cotangent, down_adapter_second)
    swapped = places.swap(cotangent)
    half = low_part.shape[1] // 2
    low_sum = places.meet(low_part[:, :half], low_part[:, half:])
    down_part, hidden, factor, act = hidden_call(gate_pre, up_pre, da)
    up, down, low_sum, down_part = barrier((up, down, low_sum, down_part))
    ups, downs = [None, up], [None, down]

    def rows_of(blocks, span):
        return [block if block is None else block[span[0] : span[0] + span[1]] for block in blocks]

    sent = places.low_send(0, low_sum, plain)
    pieces = [(0, cotangent), (1, swapped)]
    acc = None
    for hop in range(1, hops):
        last = hop == hops - 1
        if last:
            up, down = places.flood(hop + 1, *(rows_of([x[hop]], span_a)[0] for x in (ups, downs)))
        else:
            up, down = places.flood(hop + 1, ups[hop], downs[hop])
        low_sum = places.low_take(hop - 1, low_sum, sent, plain)
        sent = places.low_send(hop, low_sum, plain)
        acc = grad_call(
            "more", (0, tokens), places.table, me,
            pieces + arrived(hop - 1, places.piece(hop, ups, downs)), down_weight, acc,
        )
        pieces = []
        blocks = [up] if up is down else [up, down]
        if last:
            behind = rows_of(ups, span_b), rows_of(downs, span_b)
            blocks, acc, behind = barrier((blocks, acc, behind))
            acc, sent = barrier((acc, sent))
        else:
            blocks, acc = barrier((blocks, acc))
            acc, sent = barrier((acc, sent))
        up, down = blocks[0], blocks[-1]
        if not last:
            ups.append(up)
            downs.append(down)
    low_sum = places.low_take(hops - 1, low_sum, sent, plain)

    held = places.piece(hops, rows_of(ups, span_a) + [up], rows_of(downs, span_a) + [down])
    ups, downs = behind
    up, _ = places.flood(hops, ups[-1], downs[-1])
    low_all = jnp.concatenate(places.part(low_sum), axis=1)
    low = low_all[: 2 * rank] * BF(adapter_scale_factor)
    back = low_all[2 * rank :]
    rest = [back, da, factor, act, gate_b, up_b, low]
    early = places.dp_send(dot_nn(back, hidden), places.dp_bits(False)[0])
    part_a, second = grad_call(
        "last_a", span_a, places.table, me, arrived(hops - 1, held), down_weight, acc, rest
    )
    up, second, part_a, early = barrier((up, second, part_a, early))
    coming = places.piece(hops, ups + [up], downs + [up])
    rows = down_part.shape[0]
    before = places.meet(
        jnp.concatenate([down_part[: rows // 2], part_a[: span_a[1] // 2]], axis=0),
        jnp.concatenate([down_part[rows // 2 :], part_a[span_a[1] // 2 :]], axis=0),
    )
    before = places.send_across(before, 1)
    early = places.dp_send(summed(early), places.dp_bits(False)[1])
    part_b, *large = grad_call(
        "last_b", span_b, places.table, me, arrived(hops - 1, coming), down_weight, acc,
        rest, second, True,
    )
    part_b, before, early = barrier((part_b, before, early))

    bits = [places.dp_bits(flip) for flip in (False, True)]
    sent = [places.dp_send(x, order[0]) for x, order in zip(large, bits)]
    half = part_b.shape[0] // 2
    after = places.meet(part_b[:half], part_b[half:])
    across = places.send_across(after, 1)
    k = 2
    while k < places.chips:
        before, across, sent = barrier((before, across, sent))
        if k == 2:
            large = [summed(pair) for pair in sent]
            sent = [places.dp_send(x, order[1]) for x, order in zip(large, bits)]
        before = places.send_across(summed(before), k)
        across = places.send_across(summed(across), k)
        k *= 2
    total = jnp.concatenate([summed(before), summed(across)], axis=0).astype(BF)
    other, sent = barrier((places.swap(total), sent))
    large = [summed(pair) for pair in sent]
    sums = places.order(total, other)
    down_low = jnp.concatenate([both[: rows // 2] for both in sums], axis=0)
    down_low = jnp.concatenate(
        [down_low[i * rank : (i + 1) * rank] for i in range(tokens // LANES)], axis=1
    )
    ends = (rows // 2, rows // 2 + span_a[1] // 2)
    totals = jnp.concatenate(
        [both[ends[1] :] for both in sums] + [both[ends[0] : ends[1]] for both in sums], axis=0
    )
    firsts = jnp.concatenate([dot_tn(totals, inputs), dot_nn(down_low, cotangent)], axis=0)
    firsts = firsts * adapter_scale_factor
    grad_down_t = summed(early)
    for bit in places.dp_bits(False)[2:]:
        grad_down_t = summed(places.dp_send(grad_down_t, bit))
    for i in range(2, len(bits[0])):
        large = [summed(places.dp_send(x, order[i])) for x, order in zip(large, bits)]
    for i in range(0, len(bits[0]), 2):
        firsts = places.sum_four(firsts, bits[0][i], bits[0][i + 1])
    gate_second, up_second = large
    gate_first = firsts[:rank]
    up_first = firsts[rank : 2 * rank]
    down_second = firsts[2 * rank :]
    return (gate_first.T, gate_second, up_first.T, up_second, grad_down_t.T, down_second)


def solution(mesh):
    placed = (
        P("dp", "tensor"),
        P("dp", "tensor"),
        P("dp", "tensor"),
        P("dp", "tensor"),
        P("tensor", None),
        P("tensor", None),
        P(None, "tensor"),
        P("tensor", None),
        P(None, "tensor"),
        P("tensor", None),
        P(None, "tensor"),
    )
    return jax.shard_map(
        functools.partial(local, mesh.shape["tensor"], mesh.shape["dp"]),
        mesh=mesh,
        in_specs=placed,
        out_specs=(
            P("tensor", None),
            P(None, "tensor"),
            P("tensor", None),
            P(None, "tensor"),
            P("tensor", None),
            P(None, "tensor"),
        ),
        check_vma=False,
    )
```
